32 devices in a mesh: section: 4 (over z), expert: 8 (over y, x, core).
Axes of the slice: x: 2, y: 2, z: 4, core: 2. Of those that a mesh axis runs over, the one named last changes fastest.
Arguments:
- out_grad: bfloat16 [4, 1024, 2560], P('section', 'expert'), may hold values from -6 to 6
- expert_ids: int32 [4, 1024], P('section', 'expert'), may hold values from 0 to 3, as said below
- slot_ids: int32 [4, 1024], P('section', 'expert'), may hold values from 0 to 32, as said below
- router_logits: float32 [4, 1024, 4], P('section', 'expert'), may hold values from -8 to 8
- saved_routed: bfloat16 [4, 8, 264, 4096], P('section', 'expert'), may hold values from -6 to 6
- w_gate_up: bfloat16 [4, 8, 2560, 4096], P('section', 'expert'), may hold values from -0.125 to 0.125
- w_down: bfloat16 [4, 8, 2048, 2560], P('section', 'expert'), may hold values from -0.09375 to 0.09375
- w_router: bfloat16 [4, 2560, 4], P('section'), may hold values from -0.125 to 0.125
Outputs:
- prev_grad: bfloat16 [4, 1024, 2560], P('section', 'expert')
- routed_hgrad: bfloat16 [4, 8, 264, 4096], P('section', 'expert')
The draws below stay inside these ranges and needn't reach their ends.
Inputs may be any that keep to these rules, and one draw needn't show every extreme that they name: `expert_ids`: in each aligned block of 128 tokens of a section (one device's), one expert is named by exactly 33 tokens and every other expert by 1 to 32 tokens. `slot_ids`: within a block of 128 tokens, the number of earlier tokens of the block with the same expert.
All inputs are finite; a program needn't handle non-finite values.
Results may differ from the reference program's by a relative error of at most 0.0062.
Values may be sent and summed in bfloat16 or wider, within the bound.
No kernel may reach another device: no remote copies, remote signals or barrier semaphores. Data moves between devices by JAX's collectives and lax.ppermute only.
A program may use at most 128 MiB of HBM per device.

```python
import jax
import jax.numpy as jnp
from jax import lax

D = 2560
FF = 4096
EXPERTS = 4
TOK_DEV = 128
SECTIONS = 4
GROUP = 2
FF_DEV = 2048
TOKENS = 1024
MOST = 33
SLOTS = 264
N_EXPERT = 8


def routing_tables(key):
    blocks = SECTIONS * TOKENS // TOK_DEV

    def one_block(block_index):
        block_key = jax.random.fold_in(key, block_index)
        keys = jax.random.split(block_key, 5)
        order = jax.random.permutation(keys[0], EXPERTS)
        first = jax.random.randint(keys[1], (), 0, EXPERTS)
        second = jax.random.randint(keys[2], (), 0, EXPERTS)
        hottest = order[first * second // EXPERTS]
        shuffled = jax.random.permutation(keys[3], TOK_DEV)
        ranking = jnp.zeros((TOK_DEV,), jnp.int32).at[shuffled].set(jnp.arange(TOK_DEV, dtype=jnp.int32))
        offset = jax.random.randint(keys[4], (), 0, EXPERTS - 1)
        spread = (ranking - MOST + offset) % (EXPERTS - 1)
        others = spread + (spread >= hottest).astype(jnp.int32)
        routes = jnp.where(ranking < MOST, hottest, others).astype(jnp.int32)
        onehot = (routes[:, None] == jnp.arange(EXPERTS, dtype=jnp.int32)[None, :]).astype(jnp.int32)
        places = jnp.sum((jnp.cumsum(onehot, axis=0) - onehot) * onehot, axis=1)
        return (routes, places.astype(jnp.int32))
    routes, places = jax.vmap(one_block)(jnp.arange(blocks, dtype=jnp.int32))
    return (routes.reshape(SECTIONS, TOKENS), places.reshape(SECTIONS, TOKENS))


def draw_expert_ids(key, part):
    return routing_tables(key)[0]


def draw_slot_ids(key, part):
    return routing_tables(key)[1]


def block_scale(own_key, dims, cuts, low, largest):
    def one(position, parts):
        draws = jax.random.uniform(jax.random.fold_in(jax.random.fold_in(own_key, 6), position), (parts,), jnp.float32, low / len(cuts), largest / len(cuts))
        return jnp.repeat(jnp.exp(draws), dims[position] // parts).reshape((-1,) + (1,) * (len(dims) - position - 1))

    gain = one(*cuts[0])
    for cut in cuts[1:]:
        gain = gain * one(*cut)
    return gain


def bell_draw(stream_key, extent, width, limit, cuts=(), kind=jnp.bfloat16):
    drawn = width * jax.random.normal(stream_key, extent, jnp.float32)
    if cuts:
        drawn = drawn * block_scale(stream_key, extent, cuts, -0.22, 0.18)
    return jnp.clip(drawn, -limit, limit).astype(kind)


def setup_inputs(seed: int = 0) -> dict:
    splits = jax.random.split(jax.random.key(seed), 9)
    out_grad = bell_draw(splits[0], (SECTIONS, TOKENS, D), 1.0, 6.0, ((0, 4), (1, 8)))
    expert_ids = draw_expert_ids(jax.random.fold_in(splits[8], 71), 0)
    slot_ids = draw_slot_ids(jax.random.fold_in(splits[8], 71), 0)
    router_logits = bell_draw(splits[3], (SECTIONS, TOKENS, EXPERTS), 2.0, 8.0, ((0, 4), (1, 8)), jnp.float32)
    saved_routed = bell_draw(splits[4], (SECTIONS, EXPERTS * GROUP, SLOTS, 2 * FF_DEV), 1.0, 6.0, ((0, 4), (1, 8)))
    w_gate_up = bell_draw(splits[5], (SECTIONS, EXPERTS * GROUP, D, 2 * FF_DEV), D ** -0.5, 0.125, ((0, 4), (1, 8)))
    w_down = bell_draw(splits[6], (SECTIONS, EXPERTS * GROUP, FF_DEV, D), FF ** -0.5, 0.09375, ((0, 4), (1, 8)))
    w_router = bell_draw(splits[7], (SECTIONS, D, EXPERTS), D ** -0.5, 0.125, ((0, 4),))
    return dict(out_grad=out_grad, expert_ids=expert_ids, slot_ids=slot_ids, router_logits=router_logits, saved_routed=saved_routed, w_gate_up=w_gate_up, w_down=w_down, w_router=w_router)


def silu_parts(gate_value):
    sigm = jax.nn.sigmoid(gate_value)
    return gate_value * sigm, sigm * (1.0 + gate_value * (1.0 - sigm))


def routed_backward(slot_rows, slot_score, kept, gate_up, down):
    half = down.shape[0]
    gate_value = kept[:, :half].astype(jnp.float32)
    up_value = kept[:, half:].astype(jnp.float32)
    activated, slope = silu_parts(gate_value)
    hidden = (activated * up_value).astype(jnp.bfloat16)
    expert_out = jnp.dot(hidden, down, preferred_element_type=jnp.float32)
    inner_dot = jnp.sum(slot_rows.astype(jnp.float32) * expert_out, axis=1).astype(jnp.bfloat16)
    hidden_grad = slot_score.astype(jnp.float32)[:, None] * lax.dot_general(
        slot_rows, down, (((1,), (1,)), ((), ())), preferred_element_type=jnp.float32)
    hidden_grads = jnp.concatenate([(hidden_grad * up_value * slope).astype(jnp.bfloat16),
                                    (hidden_grad * activated).astype(jnp.bfloat16)], axis=1)
    slot_dx = lax.dot_general(hidden_grads, gate_up, (((1,), (1,)), ((), ())),
                              preferred_element_type=jnp.float32).astype(jnp.bfloat16)
    return slot_dx, inner_dot, hidden_grads


def one_section(upstream, routes, places, logits, kept_routed, gate_up, down, router_weight):
    group = N_EXPERT // EXPERTS
    source = jnp.arange(TOKENS, dtype=jnp.int32) // TOK_DEV
    target = (routes * SLOTS + source * MOST + places).astype(jnp.int32)
    onehot = routes[:, None] == jnp.arange(EXPERTS, dtype=jnp.int32)[None, :]
    chosen = jnp.sum(jnp.where(onehot, logits, jnp.float32(0.0)), axis=1)
    gate_prob = jax.nn.sigmoid(chosen)
    gating = gate_prob.astype(jnp.bfloat16)
    slot_rows = jnp.zeros((EXPERTS * SLOTS, D), jnp.bfloat16).at[target].set(upstream).reshape(EXPERTS, SLOTS, D)
    slot_score = jnp.zeros((EXPERTS * SLOTS,), jnp.bfloat16).at[target].set(gating).reshape(EXPERTS, SLOTS)

    def per_piece(pieces):
        index, kept_piece, gate_piece, down_piece = pieces
        owner = (index // group).astype(jnp.int32)
        rows = lax.dynamic_index_in_dim(slot_rows, owner, 0, keepdims=False)
        scores = lax.dynamic_index_in_dim(slot_score, owner, 0, keepdims=False)
        return routed_backward(rows, scores, kept_piece, gate_piece, down_piece)

    slot_dx, inner_dot, hidden_grads = lax.map(per_piece, (
        jnp.arange(N_EXPERT, dtype=jnp.int32), kept_routed, gate_up, down))
    summed_dx = jnp.sum(slot_dx.astype(jnp.float32).reshape(EXPERTS, group, SLOTS, D), axis=1)
    summed_inner = jnp.sum(inner_dot.astype(jnp.float32).reshape(EXPERTS, group, SLOTS), axis=1)
    returned = summed_dx.reshape(EXPERTS * SLOTS, D)[target]
    inner_tok = summed_inner.reshape(EXPERTS * SLOTS)[target]
    dlogit = gate_prob * (1.0 - gate_prob) * inner_tok
    coeffs = jnp.where(onehot, dlogit[:, None], jnp.float32(0.0))
    router_dx = jnp.dot(coeffs, router_weight.astype(jnp.float32).T, precision=lax.Precision.HIGHEST)
    summed = (returned + router_dx).astype(jnp.bfloat16)
    return summed, hidden_grads


def reference(out_grad, expert_ids, slot_ids, router_logits, saved_routed, w_gate_up, w_down, w_router):
    grads, routed_list = [], []
    for section_index in range(SECTIONS):
        summed, routed_part = one_section(
            out_grad[section_index], expert_ids[section_index], slot_ids[section_index], router_logits[section_index],
            saved_routed[section_index], w_gate_up[section_index], w_down[section_index], w_router[section_index])
        grads.append(summed)
        routed_list.append(routed_part)
    stacked = jnp.stack(grads)
    previous = jnp.concatenate([stacked[1:], jnp.zeros_like(stacked[:1])], axis=0)
    return previous, jnp.stack(routed_list)
```

```python
import functools
import math

import jax
import jax.numpy as jnp
from jax import lax
from jax.experimental import pallas as pl
from jax.experimental.pallas import tpu as pltpu
from jax.sharding import PartitionSpec as P

LANES = 128
VMEM = pl.BlockSpec(memory_space=pltpu.VMEM)
SMEM = pl.BlockSpec(memory_space=pltpu.SMEM)
HBM = pl.BlockSpec(memory_space=pltpu.HBM)
F32 = jnp.float32
BF16 = jnp.bfloat16


SCORE, SLOPE_HIGH, SLOPE_LOW, TOKEN, LAST_TOKEN = range(5)


def iota(shape, axis):
    return lax.broadcasted_iota(jnp.int32, shape, axis)


def nt_dot(a, b):
    return lax.dot_general(a, b, (((1,), (1,)), ((), ())), preferred_element_type=F32)


def one_hot(mask):
    return mask.astype(F32).astype(BF16)


def dot(a, b):
    return jnp.dot(a, b, preferred_element_type=F32)


def pack_kernel(experts, main, me, up_in, route_in, slot_in, logit_in, *refs):
    outs, refs = refs[:experts], refs[experts:]
    up_ref, route_ref, slot_ref, logit_ref, sems = refs
    copies = [
        pltpu.make_async_copy(source, target, sems.at[i])
        for i, (source, target) in enumerate(
            ((route_in, route_ref), (slot_in, slot_ref), (logit_in, logit_ref), (up_in, up_ref))
        )
    ]
    for copy in copies:
        copy.start()
    for copy in copies[:-1]:
        copy.wait()
    tokens, width = up_ref.shape
    parts = width // LANES
    route, slot = route_ref[...], slot_ref[...]
    chosen = jnp.zeros((1, tokens), F32)
    for e in range(experts):
        chosen += jnp.where(route == e, logit_ref[e : e + 1, :], 0.0)
    gate = jax.nn.sigmoid(chosen)
    slope = gate * (1.0 - gate)
    high = slope.astype(BF16).astype(F32)
    number = (iota((1, tokens), 1) + 1).astype(F32)
    turn = lax.rem(route - me[0] + experts, experts)
    place = turn * main + slot
    rows = iota((experts * main, tokens), 0)
    pick = ((rows == place) & (slot < main)).astype(F32).astype(BF16)
    top = iota((8, tokens), 0)
    last = ((top == turn) & (slot == main)).astype(F32)
    mine = (top == turn).astype(F32)
    values = jnp.concatenate(
        [mine * v for v in (gate.astype(BF16).astype(F32), high, slope - high)], axis=0
    )
    stats = nt_dot(values.astype(BF16), one_hot(iota((LANES, tokens), 0) == slot))
    by_place = one_hot((iota((LANES, tokens), 0) == place) & (slot < main))
    token = nt_dot((mine * number).astype(BF16), by_place)
    by_turn = one_hot((iota((LANES, tokens), 0) == turn) & (slot == main))
    last_token = nt_dot((mine * number).astype(BF16), by_turn)
    copies[-1].wait()
    upstream = up_ref[...]
    packed = dot(pick, upstream)
    last_rows = dot(last.astype(BF16), upstream)
    side_row = iota((main, LANES), 0)
    for k in range(experts):
        outs[k][:, :width] = packed[k * main : (k + 1) * main].astype(BF16)
        side = jnp.zeros((main, LANES), F32)
        for c in range(parts):
            side = jnp.where(side_row == c, last_rows[k : k + 1, c * LANES : (c + 1) * LANES], side)
        for c, row in (
            (SCORE, stats[k : k + 1]),
            (SLOPE_HIGH, stats[8 + k : 9 + k]),
            (SLOPE_LOW, stats[16 + k : 17 + k]),
            (TOKEN, token[k : k + 1]),
            (LAST_TOKEN, last_token[k : k + 1]),
        ):
            side = jnp.where(side_row == parts + c, row, side)
        outs[k][:, width:] = side.astype(BF16)


def arrival_row(natural, me, experts, group, main, total):
    per = main + 1
    source, slot = natural // per, lax.rem(natural, per)
    turn = lax.rem(me[0] - source // group + experts, experts)
    lane = lax.rem(lax.rem(source, group) - me[1] + group, group)
    block = lane * experts + turn
    return jnp.where(slot < main, block * main + slot, total * main + block)


def copies_of(source, first, targets, sems):
    step = targets[0].shape[0]
    return [
        pltpu.make_async_copy(source.at[(first + i) * step : (first + i + 1) * step], target, sems.at[i])
        for i, target in enumerate(targets)
    ]


def window_kernel(experts, group, main, chunks, me, kept_in, down_in, weight_in, out_ref, *refs):
    downs, weights, refs = refs[: chunks[0]], refs[chunks[0] : -4], refs[-4:]
    kept_ref, kept_sem, down_sems, weight_sems = refs
    kept_copy = pltpu.make_async_copy(kept_in, kept_ref, kept_sem)
    kept_copy.start()
    copies = copies_of(down_in, 0, downs, down_sems) + copies_of(weight_in, 0, weights, weight_sems)
    for copy in copies:
        copy.start()
    rows, columns = out_ref.shape
    place = arrival_row(iota((1, rows), 1), me, experts, group, main, experts * group)
    pick = one_hot(iota((rows, rows), 0) == place)
    kept_copy.wait()
    step = min(1024, columns)
    for c in range(0, columns, step):
        out_ref[:, c : c + step] = dot(pick, kept_ref[:, c : c + step]).astype(BF16)
    for copy in copies:
        copy.wait()


def restore_kernel(experts, group, main, me, grad_ref, out_ref):
    rows = grad_ref.shape[0]
    place = arrival_row(iota((rows, 1), 0), me, experts, group, main, experts * group)
    out_ref[...] = dot(one_hot(iota((rows, rows), 1) == place), grad_ref[...]).astype(BF16)


def silu_parts(gate_value):
    sigm = jax.nn.sigmoid(gate_value)
    return (gate_value * sigm, sigm * (1.0 + gate_value * (1.0 - sigm)))


def expert_kernel(experts, group, main, chunks, fetched, me, *refs):
    total = experts * group
    blocks, refs = refs[:total], refs[total:]
    downs, refs = refs[: chunks[0]], refs[chunks[0] :]
    weights, refs = refs[:fetched], refs[fetched:]
    kept_ref, router_ref, weight_in, grad_ref, own_ref, last_ref = refs[:6]
    sends, refs = refs[6 : 5 + group], refs[5 + group :]
    late, (rows, raw_a, raw_b, late_sems) = refs[:-4], refs[-4:]
    late_copies = copies_of(weight_in, fetched, late, late_sems)
    for copy in late_copies:
        copy.start()
    raws = (raw_a, raw_b)
    count, width = rows.shape
    parts = width // LANES
    half = kept_ref.shape[1] // 2
    full, own = total * main, experts * main

    sides = []
    for n in range(total):
        rows[n * main : (n + 1) * main, :] = blocks[n][:, :width]
        sides.append(blocks[n][:, width:])
    sides = jnp.concatenate(sides, axis=0)
    wanted = iota((parts * total, full), 0)
    pick = iota((parts * total, full), 1) == lax.rem(wanted, total) * main + wanted // total
    last = dot(one_hot(pick), sides)
    for c in range(parts):
        rows[full:, c * LANES : (c + 1) * LANES] = last[c * total : (c + 1) * total].astype(BF16)
    row = iota((count, 1), 0)
    block = jnp.where(row < full, row // main, row - full)
    slot = jnp.where(row < full, lax.rem(row, main), main)
    own_lane = iota((count, LANES), 1) == slot

    def column(which):
        choose = iota((count, full), 1) == block * main + parts + which
        return jnp.sum(jnp.where(own_lane, dot(one_hot(choose), sides), 0.0), axis=1, keepdims=True)

    score = column(SCORE)
    slope = column(SLOPE_HIGH) + column(SLOPE_LOW)
    step = raw_a.shape[1]
    inner = jnp.zeros((count, LANES), F32)

    def finish(start, raw, inner):
        piece, other = slice(start, start + step), slice(half + start, half + start + step)
        up_value = kept_ref[:, other].astype(F32)
        activated, bend = silu_parts(kept_ref[:, piece].astype(F32))
        hidden = (activated * up_value).astype(BF16).astype(F32)
        hidden_grad = score * raw
        grad_ref[:, piece] = (hidden_grad * up_value * bend).astype(BF16)
        grad_ref[:, other] = (hidden_grad * activated).astype(BF16)
        product = hidden * raw
        return inner + sum(product[:, c : c + LANES] for c in range(0, step, LANES))

    for i in range(half // step):
        raws[i % 2][...] = nt_dot(rows[...], downs[i][...])
        if i:
            inner = finish((i - 1) * step, raws[(i - 1) % 2][...], inner)
    inner = finish(half - step, raws[(half // step - 1) % 2][...], inner)
    coeff = slope * jnp.sum(inner, axis=1, keepdims=True)

    step = late[0].shape[0]
    for i, weight_ref in enumerate(list(weights) + list(late)):
        if i >= fetched:
            late_copies[i - fetched].wait()
        piece = slice(i * step, (i + 1) * step)
        router = router_ref[:, piece].astype(F32)
        router = sum(jnp.where(me[0] == e, router[e : e + 1], 0.0) for e in range(experts))
        partial = nt_dot(grad_ref[...], weight_ref[...]) + coeff * router
        last = partial[full:]
        own_ref[:, piece] = partial[:own]
        last_ref[:, piece] = last
        for lane in range(1, group):
            out = sends[lane - 1]
            out[:own, piece] = partial[lane * own : (lane + 1) * own].astype(BF16)
            out[own : own + total, piece] = last.astype(BF16)
            if out.shape[0] > own + total:
                out[own + total :, piece] = jnp.zeros((out.shape[0] - own - total, step), BF16)


def merge_kernel(experts, group, main, own_ref, last_ref, *refs):
    others = refs[: group - 1]
    sides = refs[group - 1 : group - 1 + experts]
    outs = refs[group - 1 + experts :]
    width = own_ref.shape[1]
    parts = width // LANES
    own = experts * main
    total = experts * group
    lasts = [other[own : own + total, :].astype(F32) for other in others]
    side_row = iota((main, LANES), 0)
    for k in range(experts):
        value = own_ref[k * main : (k + 1) * main, :]
        last = last_ref[k : k + 1, :]
        for lane, other in enumerate(others, 1):
            value += other[k * main : (k + 1) * main, :].astype(F32)
            row = lane * experts + k
            last += lasts[lane - 1][row : row + 1, :]
        outs[k][:, :width] = value.astype(BF16)
        side = sides[k][:, width:].astype(F32)
        for c in range(parts):
            side = jnp.where(side_row == c, last[:, c * LANES : (c + 1) * LANES], side)
        outs[k][:, width:] = side.astype(BF16)


def tokens_kernel(experts, main, *refs):
    blocks, (out_ref, rows) = refs[:experts], refs[experts:]
    tokens, width = out_ref.shape
    parts = width // LANES
    sides = []
    for k in range(experts):
        rows[k * main : (k + 1) * main, :] = blocks[k][:, :width]
        sides.append(blocks[k][:, width:])
    token = sum(side[parts + TOKEN : parts + TOKEN + 1].astype(F32) for side in sides)
    last_token = sum(side[parts + LAST_TOKEN : parts + LAST_TOKEN + 1].astype(F32) for side in sides)
    sides = jnp.concatenate(sides, axis=0)
    height = rows.shape[0] - experts * main
    wanted = iota((parts * height, experts * main), 0)
    turn = lax.rem(wanted, height)
    pick = (iota((parts * height, experts * main), 1) == turn * main + wanted // height) & (turn < experts)
    last = dot(pick.astype(F32).astype(BF16), sides)
    for c in range(parts):
        rows[experts * main :, c * LANES : (c + 1) * LANES] = last[c * height : (c + 1) * height].astype(
            BF16
        )
    number = (iota((tokens, LANES), 0) + 1).astype(F32)
    main_pick = (number == token).astype(F32).astype(BF16)
    last_pick = (number == last_token).astype(F32).astype(BF16)
    pick = jnp.concatenate([main_pick[:, : experts * main], last_pick[:, :height]], axis=1)
    out_ref[...] = dot(pick, rows[...]).astype(BF16)


def call(kernel, outs, ins, flops=0, limit=4, **options):
    ins = [
        pltpu.with_memory_space_constraint(x, pltpu.HBM) if spec is HBM else x
        for x, spec in zip(ins, options["in_specs"])
    ]
    moved = sum(math.prod(x.shape) * jnp.dtype(x.dtype).itemsize for x in list(ins) + list(outs))
    return pl.pallas_call(
        kernel,
        out_shape=tuple(outs),
        cost_estimate=pl.CostEstimate(flops=int(flops), bytes_accessed=int(moved), transcendentals=0),
        compiler_params=pltpu.CompilerParams(vmem_limit_bytes=limit * 1024 * 1024),
        **options,
    )(*ins)


def grant(scratch, more):
    return more + -(-sum(math.prod(x.shape) * jnp.dtype(x.dtype).itemsize for x in scratch) // 2**20)


def on_device(
    out_grad, expert_ids, slot_ids, router_logits, saved_routed, w_gate_up, w_down, w_router
):
    sections, total = lax.axis_size("section"), lax.axis_size("expert")
    tokens, width = out_grad.shape[1:]
    experts = router_logits.shape[2]
    group = total // experts
    capacity = saved_routed.shape[2]
    half = w_down.shape[2]
    main = capacity // total - 1
    own = experts * main
    assert own <= LANES and tokens <= 255 and width // LANES + 5 <= main and experts <= 8
    position = lax.axis_index("expert")
    me = jnp.stack([position // group, position % group]).astype(jnp.int32)
    block = jax.ShapeDtypeStruct((main, width + LANES), BF16)

    def shape(*dims, dtype=BF16):
        return jax.ShapeDtypeStruct(dims, dtype)

    def send(value, turn, lane):
        pairs = []
        for source in range(total):
            e, g = source // group, source % group
            pairs.append((source, (e + turn) % experts * group + (g - lane) % group))
        return lax.ppermute(value, "expert", pairs)

    def send_back(value, turn):
        pairs = []
        for section in range(1, sections):
            for source in range(total):
                e, g = source // group, source % group
                target = (e - turn) % experts * group + g
                pairs.append((section * total + source, (section - 1) * total + target))
        return lax.ppermute(value, ("section", "expert"), pairs)

    packed = call(
        functools.partial(pack_kernel, experts, main),
        [block] * experts,
        [me, out_grad[0], expert_ids, slot_ids, router_logits[0].T],
        2 * own * tokens * width,
        in_specs=[SMEM] + [HBM] * 4,
        out_specs=[VMEM] * experts,
        scratch_shapes=[
            pltpu.VMEM((tokens, width), BF16),
            pltpu.VMEM((1, tokens), jnp.int32),
            pltpu.VMEM((1, tokens), jnp.int32),
            pltpu.VMEM((experts, tokens), F32),
            pltpu.SemaphoreType.DMA((4,)),
        ],
    )
    held = [packed[0]] + [send(packed[k], k, 0) for k in range(1, experts)]
    first = [send(packed[0], 0, lane) for lane in range(1, group)]

    chunks = (max(1, half // 512), max(1, width // 512))
    fetched = chunks[1] - 2
    down_shape, weight_shape = (half // chunks[0], width), (width // chunks[1], 2 * half)
    ordered, *weights = call(
        functools.partial(window_kernel, experts, group, main, chunks),
        [shape(capacity, 2 * half)]
        + [pltpu.VMEM(down_shape, BF16)] * chunks[0]
        + [pltpu.VMEM(weight_shape, BF16)] * fetched,
        [me, saved_routed[0, 0], w_down[0, 0], w_gate_up[0, 0]],
        2 * capacity * capacity * 2 * half,
        8,
        in_specs=[SMEM] + [HBM] * 3,
        out_specs=[VMEM] * (1 + chunks[0] + fetched),
        scratch_shapes=[
            pltpu.VMEM((capacity, 2 * half), BF16),
            pltpu.SemaphoreType.DMA,
            pltpu.SemaphoreType.DMA((chunks[0],)),
            pltpu.SemaphoreType.DMA((fetched,)),
        ],
    )
    held[1:], ordered = lax.optimization_barrier((held[1:], ordered))
    arrived = list(held)
    rest = jnp.concatenate(held[1:], axis=0)
    for lane in range(1, group):
        other = send(rest, 0, lane)
        arrived.append(first[lane - 1])
        arrived += [other[k * main : (k + 1) * main] for k in range(experts - 1)]

    padded = own + -(-total // 16) * 16
    scratch = [pltpu.VMEM(weight_shape, BF16)] * (chunks[1] - fetched) + [
        pltpu.VMEM((capacity, width), BF16),
        pltpu.VMEM((capacity, down_shape[0]), F32),
        pltpu.VMEM((capacity, down_shape[0]), F32),
    ]
    grads, own_part, last_part, *sent = call(
        functools.partial(expert_kernel, experts, group, main, chunks, fetched),
        [
            shape(capacity, 2 * half),
            shape(own, width, dtype=F32),
            shape(total, width, dtype=F32),
        ]
        + [shape(padded, width)] * (group - 1),
        [me, *arrived]
        + [pltpu.with_memory_space_constraint(x, pltpu.VMEM) for x in weights]
        + [ordered, w_router[0].T, w_gate_up[0, 0]],
        6 * capacity * width * half,
        grant(scratch, 6),
        in_specs=[SMEM] + [VMEM] * (total + 2 + chunks[0] + fetched) + [HBM],
        out_specs=[VMEM] * (2 + group),
        scratch_shapes=scratch + [pltpu.SemaphoreType.DMA((chunks[1] - fetched,))],
    )
    others = [send(sent[lane - 1], 0, -lane) for lane in range(1, group)]

    merged = call(
        functools.partial(merge_kernel, experts, group, main),
        [block] * experts,
        [own_part, last_part] + others + held,
        own * width * group,
        in_specs=[VMEM] * (1 + group + experts),
        out_specs=[VMEM] * experts,
    )
    returned = [send_back(merged[k], k) for k in range(experts)]

    columns = min(1024, 2 * half)
    (hidden_grads,) = call(
        functools.partial(restore_kernel, experts, group, main),
        [shape(capacity, 2 * half)],
        [me, grads],
        2 * capacity * capacity * 2 * half,
        12,
        grid=(2 * half // columns,),
        in_specs=[SMEM, pl.BlockSpec((capacity, columns), lambda i: (0, i))],
        out_specs=[pl.BlockSpec((capacity, columns), lambda i: (0, i))],
    )
    (previous,) = call(
        functools.partial(tokens_kernel, experts, main),
        [shape(tokens, width)],
        returned,
        2 * own * tokens * width,
        in_specs=[VMEM] * experts,
        out_specs=[VMEM],
        scratch_shapes=[pltpu.VMEM((own + 16, width), BF16)],
    )
    return (previous[None], hidden_grads[None, None])


def solution(mesh):
    placed = (
        P("section", "expert", None),
        P("section", "expert"),
        P("section", "expert"),
        P("section", "expert", None),
        P("section", "expert", None, None),
        P("section", "expert", None, None),
        P("section", "expert", None, None),
        P("section", None, None),
    )
    return jax.shard_map(
        on_device,
        mesh=mesh,
        in_specs=placed,
        out_specs=(P("section", "expert", None), P("section", "expert", None, None)),
        check_vma=False,
    )
```

```python
import functools
import math

import jax
import jax.numpy as jnp
from jax import lax
from jax.experimental import pallas as pl
from jax.experimental.pallas import tpu as pltpu
from jax.sharding import PartitionSpec as P

LANES = 128
VMEM = pl.BlockSpec(memory_space=pltpu.VMEM)
SMEM = pl.BlockSpec(memory_space=pltpu.SMEM)
HBM = pl.BlockSpec(memory_space=pltpu.HBM)
F32 = jnp.float32
BF16 = jnp.bfloat16


SCORE, SLOPE_HIGH, SLOPE_LOW, TOKEN, LAST_TOKEN = range(5)


def iota(shape, axis):
    return lax.broadcasted_iota(jnp.int32, shape, axis)


def nt_dot(a, b):
    return lax.dot_general(a, b, (((1,), (1,)), ((), ())), preferred_element_type=F32)


def one_hot(mask):
    return mask.astype(F32).astype(BF16)


def dot(a, b):
    return jnp.dot(a, b, preferred_element_type=F32)


def pack_kernel(experts, main, me, up_in, route_in, slot_in, logit_in, *refs):
    outs, refs = refs[:experts], refs[experts:]
    up_ref, route_ref, slot_ref, logit_ref, sems = refs
    copies = [
        pltpu.make_async_copy(source, target, sems.at[i])
        for i, (source, target) in enumerate(
            ((route_in, route_ref), (slot_in, slot_ref), (logit_in, logit_ref), (up_in, up_ref))
        )
    ]
    for copy in copies:
        copy.start()
    for copy in copies[:-1]:
        copy.wait()
    tokens, width = up_ref.shape
    parts = width // LANES
    route, slot = route_ref[...], slot_ref[...]
    chosen = jnp.zeros((1, tokens), F32)
    for e in range(experts):
        chosen += jnp.where(route == e, logit_ref[e : e + 1, :], 0.0)
    gate = jax.nn.sigmoid(chosen)
    slope = gate * (1.0 - gate)
    high = slope.astype(BF16).astype(F32)
    number = (iota((1, tokens), 1) + 1).astype(F32)
    turn = lax.rem(route - me[0] + experts, experts)
    place = turn * main + slot
    rows = iota((experts * main, tokens), 0)
    pick = ((rows == place) & (slot < main)).astype(F32).astype(BF16)
    top = iota((8, tokens), 0)
    last = ((top == turn) & (slot == main)).astype(F32)
    mine = (top == turn).astype(F32)
    values = jnp.concatenate(
        [mine * v for v in (gate.astype(BF16).astype(F32), high, slope - high)], axis=0
    )
    stats = nt_dot(values.astype(BF16), one_hot(iota((LANES, tokens), 0) == slot))
    by_place = one_hot((iota((LANES, tokens), 0) == place) & (slot < main))
    token = nt_dot((mine * number).astype(BF16), by_place)
    by_turn = one_hot((iota((LANES, tokens), 0) == turn) & (slot == main))
    last_token = nt_dot((mine * number).astype(BF16), by_turn)
    copies[-1].wait()
    upstream = up_ref[...]
    packed = dot(jnp.concatenate([pick, last.astype(BF16)], axis=0), upstream)
    last_rows = packed[experts * main :]
    side_row = iota((main, LANES), 0)
    for k in range(experts):
        outs[k][:, :width] = packed[k * main : (k + 1) * main].astype(BF16)
        side = jnp.zeros((main, LANES), F32)
        for c in range(parts):
            side = jnp.where(side_row == c, last_rows[k : k + 1, c * LANES : (c + 1) * LANES], side)
        for c, row in (
            (SCORE, stats[k : k + 1]),
            (SLOPE_HIGH, stats[8 + k : 9 + k]),
            (SLOPE_LOW, stats[16 + k : 17 + k]),
            (TOKEN, token[k : k + 1]),
            (LAST_TOKEN, last_token[k : k + 1]),
        ):
            side = jnp.where(side_row == parts + c, row, side)
        outs[k][:, width:] = side.astype(BF16)


def arrival_row(natural, me, experts, group, main, total):
    per = main + 1
    source, slot = natural // per, lax.rem(natural, per)
    turn = lax.rem(me[0] - source // group + experts, experts)
    lane = lax.rem(lax.rem(source, group) - me[1] + group, group)
    block = lane * experts + turn
    return jnp.where(slot < main, block * main + slot, total * main + block)


def silu_parts(gate_value):
    sigm = jax.nn.sigmoid(gate_value)
    return (gate_value * sigm, sigm * (1.0 + gate_value * (1.0 - sigm)))


def order_kernel(experts, group, main, me, gate_ref, up_ref, hidden_ref, gate_rate_ref, up_rate_ref):
    rows = gate_ref.shape[0]
    total = experts * group
    place = arrival_row(iota((1, rows), 1), me, experts, group, main, total)
    pick = one_hot(iota((rows, rows), 0) == place)
    activated, bend = silu_parts(dot(pick, gate_ref[...]))
    up_value = dot(pick, up_ref[...])
    hidden_ref[...] = (activated * up_value).astype(BF16)
    gate_rate_ref[...] = up_value * bend
    up_rate_ref[...] = activated


def restore_kernel(experts, group, main, me, grad_ref, out_ref):
    rows = grad_ref.shape[0]
    place = arrival_row(iota((rows, 1), 0), me, experts, group, main, experts * group)
    out_ref[...] = dot(one_hot(iota((rows, rows), 1) == place), grad_ref[...]).astype(BF16)


def expert_kernel(experts, group, main, me, *refs):
    total = experts * group
    blocks, refs = refs[:total], refs[total:]
    hidden_ref, gate_rate_ref, up_rate_ref, router_ref, down_ref, weight_ref = refs[:6]
    grad_ref, own_ref, last_ref = refs[6:9]
    sends, (rows, raw_a, raw_b) = refs[9:-3], refs[-3:]
    raws = (raw_a, raw_b)
    count, width = rows.shape
    parts = width // LANES
    half = down_ref.shape[0]
    full, own = total * main, experts * main

    sides = []
    for n in range(total):
        rows[n * main : (n + 1) * main, :] = blocks[n][:, :width]
        sides.append(blocks[n][:, width:])
    sides = jnp.concatenate(sides, axis=0)
    wanted = iota((parts * total, full), 0)
    pick = iota((parts * total, full), 1) == lax.rem(wanted, total) * main + wanted // total
    last = dot(one_hot(pick), sides)
    for c in range(parts):
        rows[full:, c * LANES : (c + 1) * LANES] = last[c * total : (c + 1) * total].astype(BF16)
    def slot_columns():
        row = iota((count, 1), 0)
        block = jnp.where(row < full, row // main, row - full)
        slot = jnp.where(row < full, lax.rem(row, main), main)
        own_lane = iota((count, LANES), 1) == slot

        def column(which):
            choose = iota((count, full), 1) == block * main + parts + which
            return jnp.sum(jnp.where(own_lane, dot(one_hot(choose), sides), 0.0), axis=1, keepdims=True)

        return column(SCORE), column(SLOPE_HIGH) + column(SLOPE_LOW)

    step = raw_a.shape[1]
    inner = jnp.zeros((count, LANES), F32)

    def finish(start, raw, inner):
        piece, other = slice(start, start + step), slice(half + start, half + start + step)
        hidden_grad = score * raw
        grad_ref[:, piece] = (hidden_grad * gate_rate_ref[:, piece]).astype(BF16)
        grad_ref[:, other] = (hidden_grad * up_rate_ref[:, piece]).astype(BF16)
        product = hidden_ref[:, piece].astype(F32) * raw
        return inner + sum(product[:, c : c + LANES] for c in range(0, step, LANES))

    for i in range(half // step):
        raws[i % 2][...] = nt_dot(rows[...], down_ref[i * step : (i + 1) * step, :])
        if i == 0:
            score, slope = slot_columns()
        else:
            inner = finish((i - 1) * step, raws[(i - 1) % 2][...], inner)
    inner = finish(half - step, raws[(half // step - 1) % 2][...], inner)
    coeff = slope * jnp.sum(inner, axis=1, keepdims=True)

    step = 512 if width % 512 == 0 else LANES
    for start in range(0, width, step):
        piece = slice(start, start + step)
        router = router_ref[:, piece].astype(F32)
        router = sum(jnp.where(me[0] == e, router[e : e + 1], 0.0) for e in range(experts))
        partial = nt_dot(grad_ref[...], weight_ref[piece, :]) + coeff * router
        last = partial[full:]
        own_ref[:, piece] = partial[:own]
        last_ref[:, piece] = last
        for lane in range(1, group):
            for k in range(experts):
                out = sends[(lane - 1) * experts + k]
                first = lane * own + k * main
                out[:main, piece] = partial[first : first + main].astype(BF16)
                if k == 0:
                    out[main : main + total, piece] = last.astype(BF16)
                    if out.shape[0] > main + total:
                        out[main + total :, piece] = jnp.zeros((out.shape[0] - main - total, step), BF16)


def merge_kernel(experts, group, main, k, own_ref, last_ref, side_ref, *refs):
    others, firsts, out_ref = refs[: group - 1], refs[group - 1 : -1], refs[-1]
    width = own_ref.shape[1]
    total = experts * group
    value = own_ref[k * main : (k + 1) * main, :]
    last = last_ref[k : k + 1, :]
    for lane, (other, first) in enumerate(zip(others, firsts), 1):
        value += other[:main, :].astype(F32)
        row = lane * experts + k
        last += first[main : main + total, :].astype(F32)[row : row + 1]
    out_ref[:, :width] = value.astype(BF16)
    side = side_ref[:, width:].astype(F32)
    side_row = iota((main, LANES), 0)
    for c in range(width // LANES):
        side = jnp.where(side_row == c, last[:, c * LANES : (c + 1) * LANES], side)
    out_ref[:, width:] = side.astype(BF16)


def tokens_kernel(experts, main, *refs):
    blocks, (out, rows, out_ref, sems) = refs[:experts], refs[experts:]
    tokens, width = out_ref.shape
    parts = width // LANES
    sides = []
    for k in range(experts):
        rows[k * main : (k + 1) * main, :] = blocks[k][:, :width]
        sides.append(blocks[k][:, width:])
    token = sum(side[parts + TOKEN : parts + TOKEN + 1].astype(F32) for side in sides)
    last_token = sum(side[parts + LAST_TOKEN : parts + LAST_TOKEN + 1].astype(F32) for side in sides)
    sides = jnp.concatenate(sides, axis=0)
    height = rows.shape[0] - experts * main
    wanted = iota((parts * height, experts * main), 0)
    turn = lax.rem(wanted, height)
    pick = (iota((parts * height, experts * main), 1) == turn * main + wanted // height) & (turn < experts)
    last = dot(pick.astype(F32).astype(BF16), sides)
    for c in range(parts):
        rows[experts * main :, c * LANES : (c + 1) * LANES] = last[c * height : (c + 1) * height].astype(
            BF16
        )
    number = (iota((tokens, LANES), 0) + 1).astype(F32)
    main_pick = (number == token).astype(F32).astype(BF16)
    last_pick = (number == last_token).astype(F32).astype(BF16)
    pick = jnp.concatenate([main_pick[:, : experts * main], last_pick[:, :height]], axis=1)
    step = width // sems.shape[0]
    copies = []
    for i in range(sems.shape[0]):
        piece = slice(i * step, (i + 1) * step)
        out_ref[:, piece] = dot(pick, rows[:, piece]).astype(BF16)
        copies.append(pltpu.make_async_copy(out_ref.at[:, piece], out.at[:, piece], sems.at[i]))
        copies[-1].start()
    for copy in copies:
        copy.wait()


PACK_FLOPS = 20 * 10**9
ORDER_FLOPS = 2 * 10**9


def call(kernel, outs, ins, flops=0, limit=4, **options):
    ins = [
        pltpu.with_memory_space_constraint(x, pltpu.HBM) if spec is HBM else x
        for x, spec in zip(ins, options["in_specs"])
    ]
    moved = sum(math.prod(x.shape) * jnp.dtype(x.dtype).itemsize for x in list(ins) + list(outs))
    return pl.pallas_call(
        kernel,
        out_shape=tuple(outs),
        cost_estimate=pl.CostEstimate(flops=int(flops), bytes_accessed=int(moved), transcendentals=0),
        compiler_params=pltpu.CompilerParams(vmem_limit_bytes=limit * 1024 * 1024),
        **options,
    )(*ins)


def grant(scratch, more):
    return more + -(-sum(math.prod(x.shape) * jnp.dtype(x.dtype).itemsize for x in scratch) // 2**20)


def on_device(
    out_grad, expert_ids, slot_ids, router_logits, saved_routed, w_gate_up, w_down, w_router
):
    sections, total = lax.axis_size("section"), lax.axis_size("expert")
    tokens, width = out_grad.shape[1:]
    experts = router_logits.shape[2]
    group = total // experts
    capacity = saved_routed.shape[2]
    half = w_down.shape[2]
    main = capacity // total - 1
    own = experts * main
    assert own <= LANES and tokens <= 255 and width // LANES + 5 <= main and experts <= 8
    position = lax.axis_index("expert")
    me = jnp.stack([position // group, position % group]).astype(jnp.int32)
    block = jax.ShapeDtypeStruct((main, width + LANES), BF16)

    def shape(*dims, dtype=BF16):
        return jax.ShapeDtypeStruct(dims, dtype)

    def send(value, turn, lane):
        pairs = []
        for source in range(total):
            e, g = source // group, source % group
            pairs.append((source, (e + turn) % experts * group + (g - lane) % group))
        return lax.ppermute(value, "expert", pairs)

    def send_back(value, turn):
        pairs = []
        for section in range(1, sections):
            for source in range(total):
                e, g = source // group, source % group
                target = (e - turn) % experts * group + g
                pairs.append((section * total + source, (section - 1) * total + target))
        return lax.ppermute(value, ("section", "expert"), pairs)

    packed = call(
        functools.partial(pack_kernel, experts, main),
        [block] * experts,
        [me, out_grad[0], expert_ids, slot_ids, router_logits[0].T],
        PACK_FLOPS,
        in_specs=[SMEM] + [HBM] * 4,
        out_specs=[VMEM] * experts,
        scratch_shapes=[
            pltpu.VMEM((tokens, width), BF16),
            pltpu.VMEM((1, tokens), jnp.int32),
            pltpu.VMEM((1, tokens), jnp.int32),
            pltpu.VMEM((experts, tokens), F32),
            pltpu.SemaphoreType.DMA((4,)),
        ],
    )
    held = [packed[0]] + [send(packed[k], k, 0) for k in range(1, experts)]
    first = [send(packed[0], 0, lane) for lane in range(1, group)]

    columns = min(256, half)
    tile = pl.BlockSpec((capacity, columns), lambda i: (0, i))
    hidden, gate_rate, up_rate = call(
        functools.partial(order_kernel, experts, group, main),
        [shape(capacity, half)] + [shape(capacity, half, dtype=F32)] * 2,
        [me, saved_routed[0, 0], saved_routed[0, 0]],
        ORDER_FLOPS,
        3 + capacity * columns * 36 // 2**20,
        grid=(half // columns,),
        in_specs=[SMEM, tile, pl.BlockSpec((capacity, columns), lambda i: (0, i + half // columns))],
        out_specs=[tile] * 3,
    )
    arrived = list(held)
    for lane in range(1, group):
        arrived.append(first[lane - 1])
        for k in range(1, experts):
            value, hidden = lax.optimization_barrier((held[k], hidden))
            arrived.append(send(value, 0, lane))

    padded = main + -(-total // 16) * 16
    sent_shapes = [shape(padded, width)] + [shape(main, width)] * (experts - 1)
    step = min(256, half)
    scratch = [
        pltpu.VMEM((capacity, width), BF16),
        pltpu.VMEM((capacity, step), F32),
        pltpu.VMEM((capacity, step), F32),
    ]
    grads, own_part, last_part, *sent = call(
        functools.partial(expert_kernel, experts, group, main),
        [
            shape(capacity, 2 * half),
            shape(own, width, dtype=F32),
            shape(total, width, dtype=F32),
        ]
        + sent_shapes * (group - 1),
        [me, *arrived, hidden, gate_rate, up_rate, w_router[0].T]
        + [pltpu.with_memory_space_constraint(x[0, 0], pltpu.VMEM) for x in (w_down, w_gate_up)],
        6 * capacity * width * half,
        grant(scratch, 6),
        in_specs=[SMEM] + [VMEM] * (total + 6),
        out_specs=[VMEM] * (3 + (group - 1) * experts),
        scratch_shapes=scratch,
    )
    others = [
        [send(sent[(lane - 1) * experts + k], 0, -lane) for lane in range(1, group)]
        for k in range(experts)
    ]
    returned = []
    for k in range(experts):
        (merged,) = call(
            functools.partial(merge_kernel, experts, group, main, k),
            [block],
            [own_part, last_part, held[k], *others[k], *others[0]],
            main * width * group,
            in_specs=[VMEM] * (1 + 2 * group),
            out_specs=[VMEM],
        )
        returned.append(send_back(merged, k))

    columns = min(1024, 2 * half)
    (hidden_grads,) = call(
        functools.partial(restore_kernel, experts, group, main),
        [shape(capacity, 2 * half)],
        [me, grads],
        2 * capacity * capacity * 2 * half,
        12,
        grid=(2 * half // columns,),
        in_specs=[SMEM, pl.BlockSpec((capacity, columns), lambda i: (0, i))],
        out_specs=[pl.BlockSpec((capacity, columns), lambda i: (0, i))],
    )
    (previous,) = call(
        functools.partial(tokens_kernel, experts, main),
        [pltpu.HBM((tokens, width), BF16)],
        returned,
        2 * own * tokens * width,
        in_specs=[VMEM] * experts,
        out_specs=[HBM],
        scratch_shapes=[
            pltpu.VMEM((own + 16, width), BF16),
            pltpu.VMEM((tokens, width), BF16),
            pltpu.SemaphoreType.DMA((4 if width % (4 * LANES) == 0 else 1,)),
        ],
    )
    return (previous[None], hidden_grads[None, None])


def solution(mesh):
    placed = (
        P("section", "expert", None),
        P("section", "expert"),
        P("section", "expert"),
        P("section", "expert", None),
        P("section", "expert", None, None),
        P("section", "expert", None, None),
        P("section", "expert", None, None),
        P("section", None, None),
    )
    return jax.shard_map(
        on_device,
        mesh=mesh,
        in_specs=placed,
        out_specs=(P("section", "expert", None), P("section", "expert", None, None)),
        check_vma=False,
    )
```

```python
import functools
import math

import jax
import jax.numpy as jnp
from jax import lax
from jax.experimental import pallas as pl
from jax.experimental.pallas import tpu as pltpu
from jax.sharding import PartitionSpec as P

LANES = 128
VMEM = pl.BlockSpec(memory_space=pltpu.VMEM)
SMEM = pl.BlockSpec(memory_space=pltpu.SMEM)
HBM = pl.BlockSpec(memory_space=pltpu.HBM)
F32 = jnp.float32
BF16 = jnp.bfloat16


SCORE, SLOPE_HIGH, SLOPE_LOW, TOKEN, LAST_TOKEN = range(5)


def iota(shape, axis):
    return lax.broadcasted_iota(jnp.int32, shape, axis)


def nt_dot(a, b):
    return lax.dot_general(a, b, (((1,), (1,)), ((), ())), preferred_element_type=F32)


def one_hot(mask):
    return mask.astype(F32).astype(BF16)


def dot(a, b):
    return jnp.dot(a, b, preferred_element_type=F32)


def paired(experts):
    return experts & (experts - 1) == 0


def partner(expert, turn, experts):
    if not paired(experts):
        return (expert + turn) % experts
    return expert ^ ((turn - 2) % (experts - 1) + 1 if turn else 0)


def turn_to(source, target, experts):
    if not paired(experts):
        return lax.rem(target - source + experts, experts)
    mask = jnp.bitwise_xor(source, target)
    return jnp.where(mask > 0, lax.rem(mask, experts - 1) + 1, 0)


def pack_kernel(experts, main, me, up_in, route_in, slot_in, logit_in, *refs):
    outs, refs = refs[:experts], refs[experts:]
    up_ref, route_ref, slot_ref, logit_ref, sems = refs
    copies = [
        pltpu.make_async_copy(source, target, sems.at[i])
        for i, (source, target) in enumerate(
            ((route_in, route_ref), (slot_in, slot_ref), (logit_in, logit_ref), (up_in, up_ref))
        )
    ]
    for copy in copies:
        copy.start()
    for copy in copies[:-1]:
        copy.wait()
    tokens, width = up_ref.shape
    parts = width // LANES
    route, slot = route_ref[...], slot_ref[...]
    chosen = jnp.zeros((1, tokens), F32)
    for e in range(experts):
        chosen += jnp.where(route == e, logit_ref[e : e + 1, :], 0.0)
    gate = jax.nn.sigmoid(chosen)
    slope = gate * (1.0 - gate)
    high = slope.astype(BF16).astype(F32)
    number = (iota((1, tokens), 1) + 1).astype(F32)
    turn = turn_to(me[0], route, experts)
    place = turn * main + slot
    rows = iota((experts * main, tokens), 0)
    pick = ((rows == place) & (slot < main)).astype(F32).astype(BF16)
    top = iota((8, tokens), 0)
    last = ((top == turn) & (slot == main)).astype(F32)
    mine = (top == turn).astype(F32)
    values = jnp.concatenate(
        [mine * v for v in (gate.astype(BF16).astype(F32), high, slope - high)], axis=0
    )
    stats = nt_dot(values.astype(BF16), one_hot(iota((LANES, tokens), 0) == slot))
    by_place = one_hot((iota((LANES, tokens), 0) == place) & (slot < main))
    token = nt_dot((mine * number).astype(BF16), by_place)
    by_turn = one_hot((iota((LANES, tokens), 0) == turn) & (slot == main))
    last_token = nt_dot((mine * number).astype(BF16), by_turn)
    copies[-1].wait()
    upstream = up_ref[...]
    packed = dot(jnp.concatenate([pick, last.astype(BF16)], axis=0), upstream)
    last_rows = packed[experts * main :]
    side_row = iota((main, LANES), 0)
    for k in range(experts):
        outs[k][:, :width] = packed[k * main : (k + 1) * main].astype(BF16)
        side = jnp.zeros((main, LANES), F32)
        for c in range(parts):
            side = jnp.where(side_row == c, last_rows[k : k + 1, c * LANES : (c + 1) * LANES], side)
        for c, row in (
            (SCORE, stats[k : k + 1]),
            (SLOPE_HIGH, stats[8 + k : 9 + k]),
            (SLOPE_LOW, stats[16 + k : 17 + k]),
            (TOKEN, token[k : k + 1]),
            (LAST_TOKEN, last_token[k : k + 1]),
        ):
            side = jnp.where(side_row == parts + c, row, side)
        outs[k][:, width:] = side.astype(BF16)


def arrival_row(natural, me, experts, group, main, total):
    per = main + 1
    source, slot = natural // per, lax.rem(natural, per)
    turn = turn_to(source // group, me[0], experts)
    lane = lax.rem(lax.rem(source, group) - me[1] + group, group)
    block = lane * experts + turn
    return jnp.where(slot < main, block * main + slot, total * main + block)


def silu_parts(gate_value):
    sigm = jax.nn.sigmoid(gate_value)
    return (gate_value * sigm, sigm * (1.0 + gate_value * (1.0 - sigm)))


def order_kernel(experts, group, main, me, gate_ref, up_ref, hidden_ref, gate_rate_ref, up_rate_ref):
    rows = gate_ref.shape[0]
    total = experts * group
    place = arrival_row(iota((1, rows), 1), me, experts, group, main, total)
    pick = one_hot(iota((rows, rows), 0) == place)
    activated, bend = silu_parts(dot(pick, gate_ref[...]))
    up_value = dot(pick, up_ref[...])
    hidden_ref[...] = (activated * up_value).astype(BF16)
    gate_rate_ref[...] = up_value * bend
    up_rate_ref[...] = activated


def restore_kernel(experts, group, main, me, grad_ref, out_ref):
    rows = grad_ref.shape[0]
    place = arrival_row(iota((rows, 1), 0), me, experts, group, main, experts * group)
    out_ref[...] = dot(one_hot(iota((rows, rows), 1) == place), grad_ref[...]).astype(BF16)


def expert_kernel(experts, group, main, me, *refs):
    total = experts * group
    blocks, refs = refs[:total], refs[total:]
    hidden_ref, gate_rate_ref, up_rate_ref, router_ref, down_ref, weight_ref = refs[:6]
    grad_ref, own_ref, last_ref = refs[6:9]
    sends, (rows, raw_a, raw_b) = refs[9:-3], refs[-3:]
    raws = (raw_a, raw_b)
    count, width = rows.shape
    parts = width // LANES
    half = down_ref.shape[0]
    full, own = total * main, experts * main

    sides = []
    for n in range(total):
        rows[n * main : (n + 1) * main, :] = blocks[n][:, :width]
        sides.append(blocks[n][:, width:])
    sides = jnp.concatenate(sides, axis=0)
    wanted = iota((parts * total, full), 0)
    pick = iota((parts * total, full), 1) == lax.rem(wanted, total) * main + wanted // total
    last = dot(one_hot(pick), sides)
    for c in range(parts):
        rows[full:, c * LANES : (c + 1) * LANES] = last[c * total : (c + 1) * total].astype(BF16)
    def slot_columns():
        row = iota((count, 1), 0)
        block = jnp.where(row < full, row // main, row - full)
        slot = jnp.where(row < full, lax.rem(row, main), main)
        own_lane = iota((count, LANES), 1) == slot

        def column(which):
            choose = iota((count, full), 1) == block * main + parts + which
            return jnp.sum(jnp.where(own_lane, dot(one_hot(choose), sides), 0.0), axis=1, keepdims=True)

        return column(SCORE), column(SLOPE_HIGH) + column(SLOPE_LOW)

    step = raw_a.shape[1]
    inner = jnp.zeros((count, LANES), F32)

    def finish(start, raw, inner):
        piece, other = slice(start, start + step), slice(half + start, half + start + step)
        hidden_grad = score * raw
        grad_ref[:, piece] = (hidden_grad * gate_rate_ref[:, piece]).astype(BF16)
        grad_ref[:, other] = (hidden_grad * up_rate_ref[:, piece]).astype(BF16)
        product = hidden_ref[:, piece].astype(F32) * raw
        return inner + sum(product[:, c : c + LANES] for c in range(0, step, LANES))

    for i in range(half // step):
        raws[i % 2][...] = nt_dot(rows[...], down_ref[i * step : (i + 1) * step, :])
        if i == 0:
            score, slope = slot_columns()
        else:
            inner = finish((i - 1) * step, raws[(i - 1) % 2][...], inner)
    inner = finish(half - step, raws[(half // step - 1) % 2][...], inner)
    coeff = slope * jnp.sum(inner, axis=1, keepdims=True)

    step = 512 if width % 512 == 0 else LANES
    for start in range(0, width, step):
        piece = slice(start, start + step)
        router = router_ref[:, piece].astype(F32)
        router = sum(jnp.where(me[0] == e, router[e : e + 1], 0.0) for e in range(experts))
        partial = nt_dot(grad_ref[...], weight_ref[piece, :]) + coeff * router
        last = partial[full:]
        own_ref[:, piece] = partial[:own]
        last_ref[:, piece] = last
        for lane in range(1, group):
            for k in range(experts):
                out = sends[(lane - 1) * experts + k]
                first = lane * own + k * main
                out[:main, piece] = partial[first : first + main].astype(BF16)
                if k == 0:
                    out[main : main + total, piece] = last.astype(BF16)
                    if out.shape[0] > main + total:
                        out[main + total :, piece] = jnp.zeros((out.shape[0] - main - total, step), BF16)


def merge_kernel(experts, group, main, k, own_ref, last_ref, side_ref, *refs):
    others, firsts, out_ref = refs[: group - 1], refs[group - 1 : -1], refs[-1]
    width = own_ref.shape[1]
    total = experts * group
    value = own_ref[k * main : (k + 1) * main, :]
    last = last_ref[k : k + 1, :]
    for lane, (other, first) in enumerate(zip(others, firsts), 1):
        value += other[:main, :].astype(F32)
        row = lane * experts + k
        last += first[main : main + total, :].astype(F32)[row : row + 1]
    out_ref[:, :width] = value.astype(BF16)
    side = side_ref[:, width:].astype(F32)
    side_row = iota((main, LANES), 0)
    for c in range(width // LANES):
        side = jnp.where(side_row == c, last[:, c * LANES : (c + 1) * LANES], side)
    out_ref[:, width:] = side.astype(BF16)


def tokens_kernel(experts, main, *refs):
    blocks, (out, rows, out_ref, sems) = refs[:experts], refs[experts:]
    tokens, width = out_ref.shape
    parts = width // LANES
    sides = []
    for k in range(experts):
        rows[k * main : (k + 1) * main, :] = blocks[k][:, :width]
        sides.append(blocks[k][:, width:])
    token = sum(side[parts + TOKEN : parts + TOKEN + 1].astype(F32) for side in sides)
    last_token = sum(side[parts + LAST_TOKEN : parts + LAST_TOKEN + 1].astype(F32) for side in sides)
    sides = jnp.concatenate(sides, axis=0)
    height = rows.shape[0] - experts * main
    wanted = iota((parts * height, experts * main), 0)
    turn = lax.rem(wanted, height)
    pick = (iota((parts * height, experts * main), 1) == turn * main + wanted // height) & (turn < experts)
    last = dot(pick.astype(F32).astype(BF16), sides)
    for c in range(parts):
        rows[experts * main :, c * LANES : (c + 1) * LANES] = last[c * height : (c + 1) * height].astype(
            BF16
        )
    number = (iota((tokens, LANES), 0) + 1).astype(F32)
    main_pick = (number == token).astype(F32).astype(BF16)
    last_pick = (number == last_token).astype(F32).astype(BF16)
    pick = jnp.concatenate([main_pick[:, : experts * main], last_pick[:, :height]], axis=1)
    step = width // sems.shape[0]
    copies = []
    for i in range(sems.shape[0]):
        piece = slice(i * step, (i + 1) * step)
        out_ref[:, piece] = dot(pick, rows[:, piece]).astype(BF16)
        copies.append(pltpu.make_async_copy(out_ref.at[:, piece], out.at[:, piece], sems.at[i]))
        copies[-1].start()
    for copy in copies:
        copy.wait()


PACK_FLOPS = 20 * 10**9
ORDER_FLOPS = 2 * 10**9


def call(kernel, outs, ins, flops=0, limit=4, **options):
    ins = [
        pltpu.with_memory_space_constraint(x, pltpu.HBM) if spec is HBM else x
        for x, spec in zip(ins, options["in_specs"])
    ]
    moved = sum(math.prod(x.shape) * jnp.dtype(x.dtype).itemsize for x in list(ins) + list(outs))
    return pl.pallas_call(
        kernel,
        out_shape=tuple(outs),
        cost_estimate=pl.CostEstimate(flops=int(flops), bytes_accessed=int(moved), transcendentals=0),
        compiler_params=pltpu.CompilerParams(vmem_limit_bytes=limit * 1024 * 1024),
        **options,
    )(*ins)


def grant(scratch, more):
    return more + -(-sum(math.prod(x.shape) * jnp.dtype(x.dtype).itemsize for x in scratch) // 2**20)


def on_device(
    out_grad, expert_ids, slot_ids, router_logits, saved_routed, w_gate_up, w_down, w_router
):
    sections, total = lax.axis_size("section"), lax.axis_size("expert")
    tokens, width = out_grad.shape[1:]
    experts = router_logits.shape[2]
    group = total // experts
    capacity = saved_routed.shape[2]
    half = w_down.shape[2]
    main = capacity // total - 1
    own = experts * main
    assert own <= LANES and tokens <= 255 and width // LANES + 5 <= main and experts <= 8
    position = lax.axis_index("expert")
    me = jnp.stack([position // group, position % group]).astype(jnp.int32)
    block = jax.ShapeDtypeStruct((main, width + LANES), BF16)

    def shape(*dims, dtype=BF16):
        return jax.ShapeDtypeStruct(dims, dtype)

    def send(value, turn, lane):
        pairs = []
        for source in range(total):
            e, g = source // group, source % group
            pairs.append((source, partner(e, turn, experts) * group + (g - lane) % group))
        return lax.ppermute(value, "expert", pairs)

    def send_back(value, turn):
        origin = {partner(e, turn, experts): e for e in range(experts)}
        pairs = []
        for section in range(1, sections):
            for source in range(total):
                e, g = source // group, source % group
                target = origin[e] * group + g
                pairs.append((section * total + source, (section - 1) * total + target))
        return lax.ppermute(value, ("section", "expert"), pairs)

    packed = call(
        functools.partial(pack_kernel, experts, main),
        [block] * experts,
        [me, out_grad[0], expert_ids, slot_ids, router_logits[0].T],
        PACK_FLOPS,
        in_specs=[SMEM] + [HBM] * 4,
        out_specs=[VMEM] * experts,
        scratch_shapes=[
            pltpu.VMEM((tokens, width), BF16),
            pltpu.VMEM((1, tokens), jnp.int32),
            pltpu.VMEM((1, tokens), jnp.int32),
            pltpu.VMEM((experts, tokens), F32),
            pltpu.SemaphoreType.DMA((4,)),
        ],
    )
    held = [packed[0]] + [send(packed[k], k, 0) for k in range(1, experts)]
    first = [send(packed[0], 0, lane) for lane in range(1, group)]

    columns = min(256, half)
    tile = pl.BlockSpec((capacity, columns), lambda i: (0, i))
    hidden, gate_rate, up_rate = call(
        functools.partial(order_kernel, experts, group, main),
        [shape(capacity, half)] + [shape(capacity, half, dtype=F32)] * 2,
        [me, saved_routed[0, 0], saved_routed[0, 0]],
        ORDER_FLOPS,
        3 + capacity * columns * 36 // 2**20,
        grid=(half // columns,),
        in_specs=[SMEM, tile, pl.BlockSpec((capacity, columns), lambda i: (0, i + half // columns))],
        out_specs=[tile] * 3,
    )
    arrived = list(held)
    for lane in range(1, group):
        arrived.append(first[lane - 1])
        for k in range(1, experts):
            value, hidden = lax.optimization_barrier((held[k], hidden))
            arrived.append(send(value, 0, lane))

    padded = main + -(-total // 16) * 16
    sent_shapes = [shape(padded, width)] + [shape(main, width)] * (experts - 1)
    step = min(256, half)
    scratch = [
        pltpu.VMEM((capacity, width), BF16),
        pltpu.VMEM((capacity, step), F32),
        pltpu.VMEM((capacity, step), F32),
    ]
    grads, own_part, last_part, *sent = call(
        functools.partial(expert_kernel, experts, group, main),
        [
            shape(capacity, 2 * half),
            shape(own, width, dtype=F32),
            shape(total, width, dtype=F32),
        ]
        + sent_shapes * (group - 1),
        [me, *arrived, hidden, gate_rate, up_rate, w_router[0].T]
        + [pltpu.with_memory_space_constraint(x[0, 0], pltpu.VMEM) for x in (w_down, w_gate_up)],
        6 * capacity * width * half,
        grant(scratch, 6),
        in_specs=[SMEM] + [VMEM] * (total + 6),
        out_specs=[VMEM] * (3 + (group - 1) * experts),
        scratch_shapes=scratch,
    )
    others = [
        [send(sent[(lane - 1) * experts + k], 0, -lane) for lane in range(1, group)]
        for k in range(experts)
    ]
    returned = []
    for k in range(experts):
        (merged,) = call(
            functools.partial(merge_kernel, experts, group, main, k),
            [block],
            [own_part, last_part, held[k], *others[k], *others[0]],
            main * width * group,
            in_specs=[VMEM] * (1 + 2 * group),
            out_specs=[VMEM],
        )
        returned.append(send_back(merged, k))

    columns = min(1024, 2 * half)
    (hidden_grads,) = call(
        functools.partial(restore_kernel, experts, group, main),
        [shape(capacity, 2 * half)],
        [me, grads],
        2 * capacity * capacity * 2 * half,
        12,
        grid=(2 * half // columns,),
        in_specs=[SMEM, pl.BlockSpec((capacity, columns), lambda i: (0, i))],
        out_specs=[pl.BlockSpec((capacity, columns), lambda i: (0, i))],
    )
    (previous,) = call(
        functools.partial(tokens_kernel, experts, main),
        [pltpu.HBM((tokens, width), BF16)],
        returned,
        2 * own * tokens * width,
        in_specs=[VMEM] * experts,
        out_specs=[HBM],
        scratch_shapes=[
            pltpu.VMEM((own + 16, width), BF16),
            pltpu.VMEM((tokens, width), BF16),
            pltpu.SemaphoreType.DMA((4 if width % (4 * LANES) == 0 else 1,)),
        ],
    )
    return (previous[None], hidden_grads[None, None])


def solution(mesh):
    placed = (
        P("section", "expert", None),
        P("section", "expert"),
        P("section", "expert"),
        P("section", "expert", None),
        P("section", "expert", None, None),
        P("section", "expert", None, None),
        P("section", "expert", None, None),
        P("section", None, None),
    )
    return jax.shard_map(
        on_device,
        mesh=mesh,
        in_specs=placed,
        out_specs=(P("section", "expert", None), P("section", "expert", None, None)),
        check_vma=False,
    )
```

```python
import functools
import math

import jax
import jax.numpy as jnp
from jax import lax
from jax.experimental import pallas as pl
from jax.experimental.pallas import tpu as pltpu
from jax.sharding import PartitionSpec as P

LANES = 128
VMEM = pl.BlockSpec(memory_space=pltpu.VMEM)
SMEM = pl.BlockSpec(memory_space=pltpu.SMEM)
HBM = pl.BlockSpec(memory_space=pltpu.HBM)
F32 = jnp.float32
BF16 = jnp.bfloat16


SCORE, SLOPE_HIGH, SLOPE_LOW, TOKEN, LAST_TOKEN = range(5)


def iota(shape, axis):
    return lax.broadcasted_iota(jnp.int32, shape, axis)


def nt_dot(a, b):
    return lax.dot_general(a, b, (((1,), (1,)), ((), ())), preferred_element_type=F32)


def one_hot(mask):
    return mask.astype(F32).astype(BF16)


def dot(a, b):
    return jnp.dot(a, b, preferred_element_type=F32)


def paired(experts):
    return experts & (experts - 1) == 0


def partner(expert, turn, experts):
    if not paired(experts):
        return (expert + turn) % experts
    return expert ^ turn


def turn_to(source, target, experts):
    if not paired(experts):
        return lax.rem(target - source + experts, experts)
    return jnp.bitwise_xor(source, target)


def pack_kernel(experts, main, me, up_in, route_in, slot_in, logit_in, *refs):
    outs, refs = refs[:experts], refs[experts:]
    up_ref, route_ref, slot_ref, logit_ref, sems = refs
    copies = [
        pltpu.make_async_copy(source, target, sems.at[i])
        for i, (source, target) in enumerate(
            ((route_in, route_ref), (slot_in, slot_ref), (logit_in, logit_ref), (up_in, up_ref))
        )
    ]
    for copy in copies:
        copy.start()
    for copy in copies[:-1]:
        copy.wait()
    tokens, width = up_ref.shape
    parts = width // LANES
    route, slot = route_ref[...], slot_ref[...]
    chosen = jnp.zeros((1, tokens), F32)
    for e in range(experts):
        chosen += jnp.where(route == e, logit_ref[e : e + 1, :], 0.0)
    gate = jax.nn.sigmoid(chosen)
    slope = gate * (1.0 - gate)
    high = slope.astype(BF16).astype(F32)
    number = (iota((1, tokens), 1) + 1).astype(F32)
    turn = turn_to(me[0], route, experts)
    place = turn * main + slot
    rows = iota((experts * main, tokens), 0)
    pick = ((rows == place) & (slot < main)).astype(F32).astype(BF16)
    top = iota((8, tokens), 0)
    last = ((top == turn) & (slot == main)).astype(F32)
    mine = (top == turn).astype(F32)
    values = jnp.concatenate(
        [mine * v for v in (gate.astype(BF16).astype(F32), high, slope - high)], axis=0
    )
    stats = nt_dot(values.astype(BF16), one_hot(iota((LANES, tokens), 0) == slot))
    by_place = one_hot((iota((LANES, tokens), 0) == place) & (slot < main))
    token = nt_dot((mine * number).astype(BF16), by_place)
    by_turn = one_hot((iota((LANES, tokens), 0) == turn) & (slot == main))
    last_token = nt_dot((mine * number).astype(BF16), by_turn)
    copies[-1].wait()
    upstream = up_ref[...]
    packed = dot(jnp.concatenate([pick, last.astype(BF16)], axis=0), upstream)
    last_rows = packed[experts * main :]
    side_row = iota((main, LANES), 0)
    for k in range(experts):
        outs[k][:, :width] = packed[k * main : (k + 1) * main].astype(BF16)
        side = jnp.zeros((main, LANES), F32)
        for c in range(parts):
            side = jnp.where(side_row == c, last_rows[k : k + 1, c * LANES : (c + 1) * LANES], side)
        for c, row in (
            (SCORE, stats[k : k + 1]),
            (SLOPE_HIGH, stats[8 + k : 9 + k]),
            (SLOPE_LOW, stats[16 + k : 17 + k]),
            (TOKEN, token[k : k + 1]),
            (LAST_TOKEN, last_token[k : k + 1]),
        ):
            side = jnp.where(side_row == parts + c, row, side)
        outs[k][:, width:] = side.astype(BF16)


def arrival_row(natural, me, experts, group, main, total):
    per = main + 1
    source, slot = natural // per, lax.rem(natural, per)
    turn = turn_to(source // group, me[0], experts)
    lane = lax.rem(lax.rem(source, group) - me[1] + group, group)
    block = lane * experts + turn
    return jnp.where(slot < main, block * main + slot, total * main + block)


def silu_parts(gate_value):
    sigm = jax.nn.sigmoid(gate_value)
    return (gate_value * sigm, sigm * (1.0 + gate_value * (1.0 - sigm)))


def order_kernel(experts, group, main, me, gate_ref, up_ref, hidden_ref, gate_rate_ref, up_rate_ref):
    rows = gate_ref.shape[0]
    total = experts * group
    place = arrival_row(iota((1, rows), 1), me, experts, group, main, total)
    pick = one_hot(iota((rows, rows), 0) == place)
    activated, bend = silu_parts(dot(pick, gate_ref[...]))
    up_value = dot(pick, up_ref[...])
    hidden_ref[...] = (activated * up_value).astype(BF16)
    gate_rate_ref[...] = up_value * bend
    up_rate_ref[...] = activated


def restore_kernel(experts, group, main, me, grad_ref, out_ref):
    rows = grad_ref.shape[0]
    place = arrival_row(iota((rows, 1), 0), me, experts, group, main, experts * group)
    out_ref[...] = dot(one_hot(iota((rows, rows), 1) == place), grad_ref[...]).astype(BF16)


def expert_kernel(experts, group, main, me, *refs):
    total = experts * group
    blocks, refs = refs[:total], refs[total:]
    hidden_ref, gate_rate_ref, up_rate_ref, router_ref, down_ref, weight_ref = refs[:6]
    grad_ref, own_ref, last_ref = refs[6:9]
    sends, (rows, raw_a, raw_b) = refs[9:-3], refs[-3:]
    raws = (raw_a, raw_b)
    count, width = rows.shape
    parts = width // LANES
    half = down_ref.shape[0]
    full, own = total * main, experts * main

    sides = []
    for n in range(total):
        rows[n * main : (n + 1) * main, :] = blocks[n][:, :width]
        sides.append(blocks[n][:, width:])
    sides = jnp.concatenate(sides, axis=0)
    wanted = iota((parts * total, full), 0)
    pick = iota((parts * total, full), 1) == lax.rem(wanted, total) * main + wanted // total
    last = dot(one_hot(pick), sides)
    for c in range(parts):
        rows[full:, c * LANES : (c + 1) * LANES] = last[c * total : (c + 1) * total].astype(BF16)
    def slot_columns():
        row = iota((count, 1), 0)
        block = jnp.where(row < full, row // main, row - full)
        slot = jnp.where(row < full, lax.rem(row, main), main)
        own_lane = iota((count, LANES), 1) == slot

        def column(which):
            choose = iota((count, full), 1) == block * main + parts + which
            return jnp.sum(jnp.where(own_lane, dot(one_hot(choose), sides), 0.0), axis=1, keepdims=True)

        return column(SCORE), column(SLOPE_HIGH) + column(SLOPE_LOW)

    step = raw_a.shape[1]
    inner = jnp.zeros((count, LANES), F32)

    def finish(start, raw, inner):
        piece, other = slice(start, start + step), slice(half + start, half + start + step)
        hidden_grad = score * raw
        grad_ref[:, piece] = (hidden_grad * gate_rate_ref[:, piece]).astype(BF16)
        grad_ref[:, other] = (hidden_grad * up_rate_ref[:, piece]).astype(BF16)
        product = hidden_ref[:, piece].astype(F32) * raw
        return inner + sum(product[:, c : c + LANES] for c in range(0, step, LANES))

    for i in range(half // step):
        raws[i % 2][...] = nt_dot(rows[...], down_ref[i * step : (i + 1) * step, :])
        if i == 0:
            score, slope = slot_columns()
        else:
            inner = finish((i - 1) * step, raws[(i - 1) % 2][...], inner)
    inner = finish(half - step, raws[(half // step - 1) % 2][...], inner)
    coeff = slope * jnp.sum(inner, axis=1, keepdims=True)

    step = 512 if width % 512 == 0 else LANES
    for start in range(0, width, step):
        piece = slice(start, start + step)
        router = router_ref[:, piece].astype(F32)
        router = sum(jnp.where(me[0] == e, router[e : e + 1], 0.0) for e in range(experts))
        partial = nt_dot(grad_ref[...], weight_ref[piece, :]) + coeff * router
        last = partial[full:]
        own_ref[:, piece] = partial[:own]
        last_ref[:, piece] = last
        for lane in range(1, group):
            for k in range(experts):
                out = sends[(lane - 1) * experts + k]
                first = lane * own + k * main
                out[:main, piece] = partial[first : first + main].astype(BF16)
                if k == 0:
                    out[main : main + total, piece] = last.astype(BF16)
                    if out.shape[0] > main + total:
                        out[main + total :, piece] = jnp.zeros((out.shape[0] - main - total, step), BF16)


def merge_kernel(experts, group, main, k, own_ref, last_ref, side_ref, *refs):
    others, firsts, out_ref = refs[: group - 1], refs[group - 1 : -1], refs[-1]
    width = own_ref.shape[1]
    total = experts * group
    value = own_ref[k * main : (k + 1) * main, :]
    last = last_ref[k : k + 1, :]
    for lane, (other, first) in enumerate(zip(others, firsts), 1):
        value += other[:main, :].astype(F32)
        row = lane * experts + k
        last += first[main : main + total, :].astype(F32)[row : row + 1]
    out_ref[:, :width] = value.astype(BF16)
    side = side_ref[:, width:].astype(F32)
    side_row = iota((main, LANES), 0)
    for c in range(width // LANES):
        side = jnp.where(side_row == c, last[:, c * LANES : (c + 1) * LANES], side)
    out_ref[:, width:] = side.astype(BF16)


def tokens_kernel(experts, main, *refs):
    blocks, (out, rows, out_ref, sems) = refs[:experts], refs[experts:]
    tokens, width = out_ref.shape
    parts = width // LANES
    sides = []
    for k in range(experts):
        rows[k * main : (k + 1) * main, :] = blocks[k][:, :width]
        sides.append(blocks[k][:, width:])
    token = sum(side[parts + TOKEN : parts + TOKEN + 1].astype(F32) for side in sides)
    last_token = sum(side[parts + LAST_TOKEN : parts + LAST_TOKEN + 1].astype(F32) for side in sides)
    sides = jnp.concatenate(sides, axis=0)
    height = rows.shape[0] - experts * main
    wanted = iota((parts * height, experts * main), 0)
    turn = lax.rem(wanted, height)
    pick = (iota((parts * height, experts * main), 1) == turn * main + wanted // height) & (turn < experts)
    last = dot(pick.astype(F32).astype(BF16), sides)
    for c in range(parts):
        rows[experts * main :, c * LANES : (c + 1) * LANES] = last[c * height : (c + 1) * height].astype(
            BF16
        )
    number = (iota((tokens, LANES), 0) + 1).astype(F32)
    main_pick = (number == token).astype(F32).astype(BF16)
    last_pick = (number == last_token).astype(F32).astype(BF16)
    pick = jnp.concatenate([main_pick[:, : experts * main], last_pick[:, :height]], axis=1)
    step = width // sems.shape[0]
    copies = []
    for i in range(sems.shape[0]):
        piece = slice(i * step, (i + 1) * step)
        out_ref[:, piece] = dot(pick, rows[:, piece]).astype(BF16)
        copies.append(pltpu.make_async_copy(out_ref.at[:, piece], out.at[:, piece], sems.at[i]))
        copies[-1].start()
    for copy in copies:
        copy.wait()


PACK_FLOPS = 20 * 10**9
ORDER_FLOPS = 2 * 10**9


def call(kernel, outs, ins, flops=0, limit=4, **options):
    ins = [
        pltpu.with_memory_space_constraint(x, pltpu.HBM) if spec is HBM else x
        for x, spec in zip(ins, options["in_specs"])
    ]
    moved = sum(math.prod(x.shape) * jnp.dtype(x.dtype).itemsize for x in list(ins) + list(outs))
    return pl.pallas_call(
        kernel,
        out_shape=tuple(outs),
        cost_estimate=pl.CostEstimate(flops=int(flops), bytes_accessed=int(moved), transcendentals=0),
        compiler_params=pltpu.CompilerParams(vmem_limit_bytes=limit * 1024 * 1024),
        **options,
    )(*ins)


def grant(scratch, more):
    return more + -(-sum(math.prod(x.shape) * jnp.dtype(x.dtype).itemsize for x in scratch) // 2**20)


def on_device(
    out_grad, expert_ids, slot_ids, router_logits, saved_routed, w_gate_up, w_down, w_router
):
    sections, total = lax.axis_size("section"), lax.axis_size("expert")
    tokens, width = out_grad.shape[1:]
    experts = router_logits.shape[2]
    group = total // experts
    capacity = saved_routed.shape[2]
    half = w_down.shape[2]
    main = capacity // total - 1
    own = experts * main
    assert own <= LANES and tokens <= 255 and width // LANES + 5 <= main and experts <= 8
    position = lax.axis_index("expert")
    me = jnp.stack([position // group, position % group]).astype(jnp.int32)
    block = jax.ShapeDtypeStruct((main, width + LANES), BF16)

    def shape(*dims, dtype=BF16):
        return jax.ShapeDtypeStruct(dims, dtype)

    def send(value, turn, lane):
        pairs = []
        for source in range(total):
            e, g = source // group, source % group
            pairs.append((source, partner(e, turn, experts) * group + (g - lane) % group))
        return lax.ppermute(value, "expert", pairs)

    def send_back(value, turn):
        origin = {partner(e, turn, experts): e for e in range(experts)}
        pairs = []
        for section in range(1, sections):
            for source in range(total):
                e, g = source // group, source % group
                target = origin[e] * group + g
                pairs.append((section * total + source, (section - 1) * total + target))
        return lax.ppermute(value, ("section", "expert"), pairs)

    packed = call(
        functools.partial(pack_kernel, experts, main),
        [block] * experts,
        [me, out_grad[0], expert_ids, slot_ids, router_logits[0].T],
        PACK_FLOPS,
        in_specs=[SMEM] + [HBM] * 4,
        out_specs=[VMEM] * experts,
        scratch_shapes=[
            pltpu.VMEM((tokens, width), BF16),
            pltpu.VMEM((1, tokens), jnp.int32),
            pltpu.VMEM((1, tokens), jnp.int32),
            pltpu.VMEM((experts, tokens), F32),
            pltpu.SemaphoreType.DMA((4,)),
        ],
    )
    held = [packed[0]] + [send(packed[k], k, 0) for k in range(1, experts)]
    first = [send(packed[0], 0, lane) for lane in range(1, group)]

    columns = min(256, half)
    tile = pl.BlockSpec((capacity, columns), lambda i: (0, i))
    hidden, gate_rate, up_rate = call(
        functools.partial(order_kernel, experts, group, main),
        [shape(capacity, half)] + [shape(capacity, half, dtype=F32)] * 2,
        [me, saved_routed[0, 0], saved_routed[0, 0]],
        ORDER_FLOPS,
        3 + capacity * columns * 36 // 2**20,
        grid=(half // columns,),
        in_specs=[SMEM, tile, pl.BlockSpec((capacity, columns), lambda i: (0, i + half // columns))],
        out_specs=[tile] * 3,
    )
    arrived = list(held)
    for lane in range(1, group):
        arrived.append(first[lane - 1])
        for k in range(1, experts):
            value, hidden = lax.optimization_barrier((held[k], hidden))
            arrived.append(send(value, 0, lane))

    padded = main + -(-total // 16) * 16
    sent_shapes = [shape(padded, width)] + [shape(main, width)] * (experts - 1)
    step = min(256, half)
    scratch = [
        pltpu.VMEM((capacity, width), BF16),
        pltpu.VMEM((capacity, step), F32),
        pltpu.VMEM((capacity, step), F32),
    ]
    grads, own_part, last_part, *sent = call(
        functools.partial(expert_kernel, experts, group, main),
        [
            shape(capacity, 2 * half),
            shape(own, width, dtype=F32),
            shape(total, width, dtype=F32),
        ]
        + sent_shapes * (group - 1),
        [me, *arrived, hidden, gate_rate, up_rate, w_router[0].T]
        + [pltpu.with_memory_space_constraint(x[0, 0], pltpu.VMEM) for x in (w_down, w_gate_up)],
        6 * capacity * width * half,
        grant(scratch, 6),
        in_specs=[SMEM] + [VMEM] * (total + 6),
        out_specs=[VMEM] * (3 + (group - 1) * experts),
        scratch_shapes=scratch,
    )
    others, returned = {}, {}
    back = [0, experts - 1, *range(1, experts - 1)]
    for k in back:
        others[k] = [send(sent[(lane - 1) * experts + k], 0, -lane) for lane in range(1, group)]
    for k in back:
        (merged,) = call(
            functools.partial(merge_kernel, experts, group, main, k),
            [block],
            [own_part, last_part, held[k], *others[k], *others[0]],
            main * width * group,
            in_specs=[VMEM] * (1 + 2 * group),
            out_specs=[VMEM],
        )
        returned[k] = send_back(merged, k)
    returned = [returned[k] for k in range(experts)]

    columns = min(1024, 2 * half)
    (hidden_grads,) = call(
        functools.partial(restore_kernel, experts, group, main),
        [shape(capacity, 2 * half)],
        [me, grads],
        2 * capacity * capacity * 2 * half,
        12,
        grid=(2 * half // columns,),
        in_specs=[SMEM, pl.BlockSpec((capacity, columns), lambda i: (0, i))],
        out_specs=[pl.BlockSpec((capacity, columns), lambda i: (0, i))],
    )
    (previous,) = call(
        functools.partial(tokens_kernel, experts, main),
        [pltpu.HBM((tokens, width), BF16)],
        returned,
        2 * own * tokens * width,
        in_specs=[VMEM] * experts,
        out_specs=[HBM],
        scratch_shapes=[
            pltpu.VMEM((own + 16, width), BF16),
            pltpu.VMEM((tokens, width), BF16),
            pltpu.SemaphoreType.DMA((4 if width % (4 * LANES) == 0 else 1,)),
        ],
    )
    return (previous[None], hidden_grads[None, None])


def solution(mesh):
    placed = (
        P("section", "expert", None),
        P("section", "expert"),
        P("section", "expert"),
        P("section", "expert", None),
        P("section", "expert", None, None),
        P("section", "expert", None, None),
        P("section", "expert", None, None),
        P("section", None, None),
    )
    return jax.shard_map(
        on_device,
        mesh=mesh,
        in_specs=placed,
        out_specs=(P("section", "expert", None), P("section", "expert", None, None)),
        check_vma=False,
    )
```
